32 devices in a mesh: groups: 2 (over x), replica: 4 (over z), tensor: 4 (over y, core).
Axes of the slice: x: 2, y: 2, z: 4, core: 2. Of those that a mesh axis runs over, the one named last changes fastest.
Arguments:
- queries: bfloat16 [2, 512, 8192], P(None, ('groups', 'replica'), 'tensor'), parts along dimension 1, may hold values from -6 to 6
- new_kv: bfloat16 [2, 512, 8, 256], P(None, ('groups', 'replica'), 'tensor'), parts along dimension 1, may hold values from -6 to 6, as said below
- pool: bfloat16 [5120, 16, 8, 256], P(('groups', 'replica'), None, 'tensor'), parts along dimension 0, may hold values from -6 to 6, as said below
- lengths: int32 [512], P(('groups', 'replica')), parts along dimension 0, may hold values from 0 to 160, as said below
- block_table: int32 [512, 10], P(('groups', 'replica')), parts along dimension 0, may hold values from 0 to 639, as said below
- plan: int32 [8, 4], P('groups'), parts along dimension 0, may hold values from 0 to 63, as said below
- w_out: bfloat16 [8192, 8192], P('tensor'), may hold values from -0.75 to 0.75
- residual: bfloat16 [2, 512, 8192], P(None, ('groups', 'replica')), parts along dimension 1, may hold values from -30 to 30
- norm_gain: bfloat16 [8192], replicated, may hold values from 0.099609375 to 1.8984375
Outputs:
- hidden: bfloat16 [2, 512, 8192], P(None, ('groups', 'replica')), parts along dimension 1
- normed: bfloat16 [2, 512, 8192], P(None, ('groups', 'replica')), parts along dimension 1
The draws below stay inside these ranges and needn't reach their ends.
There are 2 independent parts, one for each index of `groups`. The reference program is written for one: setup_inputs(seed, part) draws one part's arguments, and reference() takes and returns one part's arrays. A program takes and returns all parts, laid end to end along the dimension named above; an argument that names none is the same for every part. Nothing has to cross between parts.
Inputs may be any that keep to these rules, and one draw needn't show every extreme that they name: `lengths`: 0 marks a free slot; a moved request of 160 tokens occurs in every draw. `plan`: half of the replicas are sources and half destinations; each source gives exactly 2 live requests, each destination takes exactly 2 into distinct free slots; no two rows share both source and destination. `block_table`: the first ceil(lengths[n] / 16) entries of a row are distinct blocks of the replica; the other entries are 0. `pool`: copies c and c' with c * 1 = c' * 8 // 8 are equal. `new_kv`: copies of one key-value head are equal, as in pool.
All inputs are finite; a program needn't handle non-finite values.
Results may differ from the reference program's by a relative error of at most 0.0062.
Values may be sent and summed in bfloat16 or wider, within the bound.
A program may use at most 192 MiB of HBM per device.

```python
import math
import jax
import jax.numpy as jnp
from jax import lax

D = 8192
HEADS = 64
KVH = 8
HD = 128
ROWS = 64
MAXBLK = 10
BLK = 16
STEPS = 2
SEND = 2
MIG = 4
BLOCKS = 640
MAXLEN = 160
KVS = 8
N_REPLICA = 4


def plan_layout(key):
    replicas = N_REPLICA
    halves = replicas // 2
    shuffle = jax.random.permutation(jax.random.fold_in(key, 11), replicas).astype(jnp.int32)
    loaded = shuffle[:halves]
    lighter = shuffle[halves:]
    moves = jnp.arange(MIG, dtype=jnp.int32)
    column = moves // SEND
    within = moves % SEND
    source = loaded[column]
    target = lighter[(column + within) % halves]

    def shuffled(sub_key):
        return jax.random.permutation(sub_key, ROWS)
    slot_order = jax.vmap(shuffled)(jax.random.split(jax.random.fold_in(key, 12), replicas)).astype(jnp.int32)
    source_slot = slot_order[source, within]
    target_slot = slot_order[target, within]
    long_len = jax.random.randint(jax.random.fold_in(key, 13), (replicas, ROWS), MAXLEN // 2, MAXLEN + 1)
    short_len = jax.random.randint(jax.random.fold_in(key, 14), (replicas, ROWS), 1, MAXLEN // 3 + 1)
    heavy = jnp.zeros((replicas,), dtype=bool).at[loaded].set(True)
    lengths = jnp.where(heavy[:, None], long_len, short_len).astype(jnp.int32)
    lengths = lengths.at[target, target_slot].set(0)
    lengths = lengths.at[source[0], source_slot[0]].set(MAXLEN)

    def block_order(sub_key):
        return jax.random.permutation(sub_key, BLOCKS)
    block_perm = jax.vmap(block_order)(jax.random.split(jax.random.fold_in(key, 15), replicas)).astype(jnp.int32)
    block_perm = block_perm.reshape(replicas, ROWS, MAXBLK)
    needed = (lengths + BLK - 1) // BLK
    table = jnp.where(jnp.arange(MAXBLK, dtype=jnp.int32)[None, None, :] < needed[:, :, None], block_perm, 0)
    plan = jnp.stack([source_slot, source, target, target_slot], axis=1).astype(jnp.int32)
    return (lengths.reshape(replicas * ROWS), plan, table.reshape(replicas * ROWS, MAXBLK).astype(jnp.int32))


def draw_lengths(key, part):
    lengths, plan, table = plan_layout(key)
    return lengths


def draw_plan(key, part):
    lengths, plan, table = plan_layout(key)
    return plan


def draw_block_table(key, part):
    lengths, plan, table = plan_layout(key)
    return table


def draw_pool(key, part):
    key = jax.random.fold_in(key, 4)
    base_key = jax.random.fold_in(key, 0)
    shape = (N_REPLICA * BLOCKS, BLK, KVH, 2 * HD)
    values = jnp.clip(jax.random.normal(base_key, shape, jnp.float32), -6.0, 6.0)
    return jnp.repeat(values, KVS // KVH, axis=2).astype(jnp.bfloat16)


def draw_new_kv(key, part):
    key = jax.random.fold_in(key, 5)
    base_key = jax.random.fold_in(key, 0)
    shape = (STEPS, N_REPLICA * ROWS, KVH, 2 * HD)
    values = jnp.clip(jax.random.normal(base_key, shape, jnp.float32), -6.0, 6.0)
    return jnp.repeat(values, KVS // KVH, axis=2).astype(jnp.bfloat16)


def draw_queries(key, part):
    key = jax.random.fold_in(key, 6)
    base_key = jax.random.fold_in(key, 0)
    shape = (STEPS, N_REPLICA * ROWS, KVH, HEADS // KVH, HD)
    values = jnp.clip(jax.random.normal(base_key, shape, jnp.float32), -6.0, 6.0)
    return values.reshape(STEPS, N_REPLICA * ROWS, HEADS * HD).astype(jnp.bfloat16)


def draw_residual(key, part):
    key = jax.random.fold_in(key, 7)
    row_key, column_key, base_key = jax.random.split(key, 3)
    shape = (STEPS, N_REPLICA * ROWS, D)
    row_scale = jnp.exp(jax.random.uniform(row_key, (STEPS, N_REPLICA * ROWS, 1), jnp.float32, jnp.log(0.2), jnp.log(2.0)))
    rough = jnp.exp(jax.random.uniform(column_key, (D,), jnp.float32, jnp.log(0.4), jnp.log(2.0)))
    ramp = jnp.arange(D, dtype=jnp.float32) / (D - 1)
    base = jnp.clip(jax.random.normal(base_key, shape, jnp.float32), -3.0, 3.0)
    rising = jnp.exp(ramp * jnp.log(2.0))
    return jnp.clip(base * row_scale * rough * rising, -30.0, 30.0).astype(jnp.bfloat16)


def raised(entries, own_key, source, target, blocks, factor):
    def block_of(axis_at):
        return (jnp.arange(entries.shape[axis_at]) // (entries.shape[axis_at] // blocks)).reshape((-1,) + (1,) * (entries.ndim - 1 - axis_at))

    first = jax.random.permutation(own_key, blocks)[block_of(target)]
    far = (block_of(target) + blocks // 2) % blocks
    return jnp.where((block_of(source) == first) | (block_of(source) == far), factor * entries, entries)


def levels(rng, extent, shards, low, high):
    def one(position, shards_of):
        steps = jax.random.uniform(jax.random.fold_in(jax.random.fold_in(rng, 6), position), (shards_of,), jnp.float32, low / len(shards), high / len(shards))
        return jnp.repeat(jnp.exp(steps), extent[position] // shards_of).reshape((-1,) + (1,) * (len(extent) - position - 1))

    factor_of = one(*shards[0])
    for cut in shards[1:]:
        factor_of = factor_of * one(*cut)
    return factor_of


def bell_draw_with(rng, dims, spread, bound, pieces, heavy, kind=jnp.bfloat16):
    entries = spread * jax.random.normal(rng, dims, jnp.float32)
    if pieces:
        entries = entries * levels(rng, dims, pieces, -0.22, 0.18)
    return jnp.clip(raised(entries, jax.random.fold_in(rng, 3), *heavy), -bound, bound).astype(kind)


def setup_inputs(seed: int = 0, part: int = 0) -> dict:
    key_list = jax.random.split(jax.random.key(seed), 10)
    part_keys = jax.random.split(jax.random.fold_in(key_list[9], part), 10)
    return {
        "queries": draw_queries(jax.random.fold_in(jax.random.fold_in(key_list[9], part), 71), part),
        "new_kv": draw_new_kv(jax.random.fold_in(jax.random.fold_in(key_list[9], part), 71), part),
        "pool": draw_pool(jax.random.fold_in(jax.random.fold_in(key_list[9], part), 71), part),
        "lengths": draw_lengths(jax.random.fold_in(jax.random.fold_in(key_list[9], part), 71), part),
        "block_table": draw_block_table(jax.random.fold_in(jax.random.fold_in(key_list[9], part), 71), part),
        "plan": draw_plan(jax.random.fold_in(jax.random.fold_in(key_list[9], part), 71), part),
        "w_out": bell_draw_with(key_list[6], (HEADS * HD, D), HD ** -0.5, 0.75, ((0, 4),), (0, 1, 4, 2.0)),
        "residual": draw_residual(jax.random.fold_in(jax.random.fold_in(key_list[9], part), 71), part),
        "norm_gain": jnp.clip(1.0 + 0.18 * jax.random.normal(key_list[8], (D,), jnp.float32), 0.099609375, 1.8984375).astype(jnp.bfloat16),
    }


def route_rows(lengths, plan):
    total_rows = lengths.shape[0]
    slot_ids = jnp.arange(total_rows, dtype=jnp.int32)
    source_row = plan[:, 1] * ROWS + plan[:, 0]
    target_row = plan[:, 2] * ROWS + plan[:, 3]
    hit_in = slot_ids[:, None] == target_row[None, :]
    incoming = jnp.any(hit_in, axis=1)
    home_row = jnp.where(incoming, lax.optimization_barrier(jnp.sum(jnp.where(hit_in, source_row[None, :], 0), axis=1)), slot_ids).astype(jnp.int32)
    moved_out = jnp.any(slot_ids[:, None] == source_row[None, :], axis=1)
    live_rows = incoming | (lengths > 0) & jnp.logical_not(moved_out)
    return (home_row, lengths[home_row], live_rows)

def attend(query_block, fresh_rows, cache_rows, live_count):
    head_dim = query_block.shape[-1]
    inv_root = 1.0 / math.sqrt(head_dim)
    query_wide = query_block.astype(jnp.float32)
    past_keys = cache_rows[..., :head_dim].astype(jnp.float32)
    past_values = cache_rows[..., head_dim:].astype(jnp.float32)
    new_keys = fresh_rows[..., :head_dim].astype(jnp.float32)
    new_values = fresh_rows[..., head_dim:].astype(jnp.float32)
    past_scores = jnp.einsum('snkgd,npkd->snkgp', query_wide, past_keys) * inv_root
    fresh_scores = jnp.einsum('snkgd,tnkd->snkgt', query_wide, new_keys) * inv_root
    places = jnp.arange(cache_rows.shape[1], dtype=jnp.int32)
    seen = places[None, :] < live_count[:, None]
    past_scores = jnp.where(seen[None, :, None, None, :], past_scores, -jnp.inf)
    step_ids = jnp.arange(query_block.shape[0], dtype=jnp.int32)
    causal_mask = step_ids[:, None] >= step_ids[None, :]
    fresh_scores = jnp.where(causal_mask[:, None, None, None, :], fresh_scores, -jnp.inf)
    highest = jnp.maximum(lax.optimization_barrier(jnp.max(past_scores, axis=-1)), lax.optimization_barrier(jnp.max(fresh_scores, axis=-1)))
    past_exp = jnp.exp(past_scores - highest[..., None])
    fresh_exp = jnp.exp(fresh_scores - highest[..., None])
    denominator = lax.optimization_barrier(jnp.sum(past_exp, axis=-1)) + lax.optimization_barrier(jnp.sum(fresh_exp, axis=-1))
    past_weights = (past_exp / denominator[..., None]).astype(jnp.bfloat16)
    fresh_weights = (fresh_exp / denominator[..., None]).astype(jnp.bfloat16)
    head_sum = jnp.einsum('snkgp,npkd->snkgd', past_weights.astype(jnp.float32), past_values)
    head_sum = head_sum + jnp.einsum('snkgt,tnkd->snkgd', fresh_weights.astype(jnp.float32), new_values)
    return head_sum.astype(jnp.bfloat16)

def finish(mixed_sum, resid_rows, keep_rows, gain_vector):
    full_sum = jnp.where(keep_rows[:, None], resid_rows.astype(jnp.float32) + mixed_sum, 0.0)
    hidden = full_sum.astype(jnp.bfloat16)
    widened = lax.optimization_barrier(hidden).astype(jnp.float32)
    mean_square = lax.optimization_barrier(jnp.mean(widened * widened, axis=-1, keepdims=True))
    normed = (widened * lax.rsqrt(mean_square + 1e-05) * gain_vector.astype(jnp.float32)).astype(jnp.bfloat16)
    return (hidden, normed)

def reference(queries, new_kv, pool, lengths, block_table, plan, w_out, residual, norm_gain):
    home_row, live_count, live_rows = route_rows(lengths, plan)
    step_count = queries.shape[0]
    group_size = HEADS // KVH
    copy_stride = KVS // KVH

    def one_replica(replica_id):
        first_row = replica_id * ROWS
        own_home = lax.dynamic_slice_in_dim(home_row, first_row, ROWS)
        table_rows = block_table[own_home] + (own_home // ROWS * BLOCKS)[:, None]
        cache_rows = pool[table_rows][:, :, :, ::copy_stride, :].reshape(ROWS, MAXBLK * BLK, KVH, 2 * HD)
        query_block = lax.dynamic_slice_in_dim(queries, first_row, ROWS, 1).reshape(step_count, ROWS, KVH, group_size, HD)
        fresh_rows = lax.dynamic_slice_in_dim(new_kv, first_row, ROWS, 1)[:, :, ::copy_stride, :]
        own_count = lax.dynamic_slice_in_dim(live_count, first_row, ROWS)
        return attend(query_block, fresh_rows, cache_rows, own_count)
    head_out = lax.map(one_replica, jnp.arange(N_REPLICA, dtype=jnp.int32))
    head_out = jnp.transpose(head_out, (1, 0, 2, 3, 4, 5)).reshape(step_count * N_REPLICA * ROWS, HEADS * HD)
    mixed_sum = jnp.dot(head_out, w_out, preferred_element_type=jnp.float32)
    keep_rows = jnp.tile(live_rows, step_count)
    hidden, normed = finish(mixed_sum, residual.reshape(step_count * N_REPLICA * ROWS, D), keep_rows, norm_gain)
    out_shape = (step_count, N_REPLICA * ROWS, D)
    return (hidden.reshape(out_shape), normed.reshape(out_shape))
```

```python
import functools
import math

import jax
import jax.numpy as jnp
from jax import lax
from jax.experimental import pallas as pl
from jax.experimental.pallas import tpu as pltpu
from jax.sharding import PartitionSpec as P

SEND = 2
CHUNK = 512
MESH = pl.DeviceIdType.MESH
VMEM = pl.BlockSpec(memory_space=pltpu.VMEM)
ANY = pl.BlockSpec(memory_space=pl.ANY)
SMEM = pl.BlockSpec(memory_space=pltpu.SMEM)


def attend_kernel(dims, table_ref, count_ref, query_ref, fresh_ref, pool_ref, out_ref, keys, values, sems):
    slots, blocks, steps, heads, copies, unroll = dims
    head_dim = query_ref.shape[-1]
    rows = steps * heads
    block_rows = keys.shape[1] * copies
    cached = blocks * block_rows
    fresh_pad = fresh_ref.shape[1]
    total = cached + fresh_pad
    get_keys = pltpu.make_async_copy(pool_ref.at[..., pl.ds(0, head_dim)], keys, sems.at[0])
    get_values = pltpu.make_async_copy(pool_ref.at[..., pl.ds(head_dim, head_dim)], values, sems.at[1])
    get_keys.start()
    get_values.start()
    inv_root = 1.0 / math.sqrt(head_dim)
    row = lax.broadcasted_iota(jnp.int32, (rows, total), 0)
    col = lax.broadcasted_iota(jnp.int32, (rows, total), 1)
    step = row // heads
    copy = (row % heads) // (heads // copies)
    is_fresh = col >= cached
    fresh_step = (col - cached) // copies
    same_copy = (col % copies) == copy
    fresh_ok = is_fresh & same_copy & (fresh_step <= step)
    old_limit = jnp.where(is_fresh | jnp.logical_not(same_copy), 1 << 20, col)
    get_keys.wait()
    get_values.wait()

    def one(n):
        kk = [keys[table_ref[n * blocks + b]].reshape(block_rows, head_dim) for b in range(blocks)]
        vv = [values[table_ref[n * blocks + b]].reshape(block_rows, head_dim) for b in range(blocks)]
        new = fresh_ref[n]
        kk = jnp.concatenate(kk + [new[:, :head_dim]], axis=0)
        vv = jnp.concatenate(vv + [new[:, head_dim:]], axis=0)
        scores = lax.dot_general(
            query_ref[n], kk, (((1,), (1,)), ((), ())), preferred_element_type=jnp.float32
        ) * inv_root
        ok = fresh_ok | (old_limit < count_ref[n] * copies)
        scores = jnp.where(ok, scores, -jnp.inf)
        top = jnp.max(scores, axis=-1, keepdims=True)
        powers = jnp.exp(scores - top)
        denominator = jnp.sum(powers, axis=-1, keepdims=True)
        weights = (powers / denominator).astype(jnp.bfloat16)
        out_ref[n] = jnp.dot(weights, vv, preferred_element_type=jnp.float32).astype(jnp.bfloat16)

    def body(i, carry):
        for u in range(unroll):
            one(i * unroll + u)
        return carry

    lax.fori_loop(0, slots // unroll, body, 0)


def attend(query_rows, fresh_rows, pool, table, count, steps, copies):
    slots, rows, head_dim = query_rows.shape
    blocks = table.shape[1]
    if copies == 1:
        pool = pool.reshape(pool.shape[0], pool.shape[1], pool.shape[3])
    unroll = 4 if slots % 4 == 0 else 1
    dims = (slots, blocks, steps, rows // steps, copies, unroll)
    part = pool.shape[:-1] + (head_dim,)
    return pl.pallas_call(
        functools.partial(attend_kernel, dims),
        out_shape=jax.ShapeDtypeStruct((slots, rows, head_dim), jnp.bfloat16),
        in_specs=[SMEM, SMEM, VMEM, VMEM, ANY],
        out_specs=VMEM,
        scratch_shapes=[
            pltpu.VMEM(part, jnp.bfloat16),
            pltpu.VMEM(part, jnp.bfloat16),
            pltpu.SemaphoreType.DMA((2,)),
        ],
        compiler_params=pltpu.CompilerParams(vmem_limit_bytes=40 * 2**20),
        cost_estimate=pl.CostEstimate(
            flops=4 * slots * rows * 336 * head_dim, bytes_accessed=4 * pool.size, transcendentals=slots * rows * 336
        ),
    )(table.reshape(-1), count, query_rows, fresh_rows, pool)


def pack_kernel(blocks, table_ref, chosen_ref, size_ref, pool_ref, out_ref, note, sems):
    copies = []
    for j in range(SEND):
        for b in range(blocks):
            copies.append(
                pltpu.make_async_copy(
                    pool_ref.at[table_ref[chosen_ref[j] * blocks + b]],
                    out_ref.at[j * (blocks + 1) + b],
                    sems.at[j * (blocks + 1) + b],
                )
            )
            copies[-1].start()
    for j in range(SEND):
        size = jnp.full(note.shape[1:], size_ref[j], jnp.int32)
        note[j] = size.astype(jnp.float32).astype(jnp.bfloat16)
        at = j * (blocks + 1) + blocks
        copies.append(pltpu.make_async_copy(note.at[j], out_ref.at[at], sems.at[at]))
        copies[-1].start()
    for copy in copies:
        copy.wait()


def pack(pool, table, chosen, sizes):
    blocks = table.shape[1]
    count = SEND * (blocks + 1)
    return pl.pallas_call(
        functools.partial(pack_kernel, blocks),
        out_shape=jax.ShapeDtypeStruct((count,) + pool.shape[1:], pool.dtype),
        in_specs=[SMEM, SMEM, SMEM, ANY],
        out_specs=ANY,
        scratch_shapes=[
            pltpu.VMEM((SEND,) + pool.shape[1:], pool.dtype),
            pltpu.SemaphoreType.DMA((count,)),
        ],
    )(table.reshape(-1), chosen, sizes, pool)


def project_kernel(ranks, head_ref, keep_ref, gain_ref, resid_ref, w_ref, hidden_ref, normed_ref,
                   weight, sib_out, sib_in, y_out, y_in, whole, w_sem, s_send, s_recv, y_send, y_recv,
                   g_send, g_recv, h_send, h_recv):
    rows, width = hidden_ref.shape
    tall = ranks // 2
    pieces = width // ranks // CHUNK
    me = lax.axis_index("tensor")
    level = me // 2
    core = me % 2
    sibling = level * 2 + 1 - core

    def place(side, at_level, k):
        return (side * tall + at_level) * pieces + k

    def peer(off):
        return lax.rem(level + off, tall) * 2 + core

    barrier = pltpu.get_barrier_semaphore()
    pl.semaphore_signal(barrier, inc=1, device_id={"tensor": sibling}, device_id_type=MESH)
    for off in range(1, tall):
        pl.semaphore_signal(barrier, inc=1, device_id={"tensor": peer(off)}, device_id_type=MESH)

    def fetch(i, side):
        at_level = lax.rem(level + 1 + i // pieces, tall)
        chunk = place(side, at_level, lax.rem(i, pieces))
        slot = i * 2 + (0 if side is sib_side else 1)
        return pltpu.make_async_copy(
            w_ref.at[:, pl.ds(pl.multiple_of(chunk * CHUNK, CHUNK), CHUNK)], weight.at[slot], w_sem.at[slot]
        )

    sib_side = 1 - core
    steps = tall * pieces

    def start_fetch(i, carry):
        fetch(i, sib_side).start()
        fetch(i, core).start()
        return carry

    lax.fori_loop(0, steps, start_fetch, 0)
    pl.semaphore_wait(barrier, tall)

    def to_sibling(i):
        return pltpu.make_async_remote_copy(
            sib_out.at[i], sib_in.at[i], s_send.at[i], s_recv.at[i],
            device_id={"tensor": sibling}, device_id_type=MESH)

    def to_peer(i):
        off = 1 + i // pieces
        return pltpu.make_async_remote_copy(
            y_out.at[i], y_in.at[i], y_send.at[i], y_recv.at[i],
            device_id={"tensor": peer(off)}, device_id_type=MESH)

    def gather_peer(off, k):
        at = (off - 1) * pieces + k
        slot = place(core, level, k)
        return pltpu.make_async_remote_copy(
            whole.at[slot], whole.at[slot], g_send.at[at], g_recv.at[at],
            device_id={"tensor": peer(off)}, device_id_type=MESH)

    def gather_wait(off, k):
        at = (off - 1) * pieces + k
        slot = place(core, lax.rem(level + tall - off, tall), k)
        return slot, pltpu.make_async_remote_copy(
            whole.at[slot], whole.at[slot], g_send.at[at], g_recv.at[at],
            device_id={"tensor": peer(off)}, device_id_type=MESH)

    def hand_over(side, off, k):
        at = off * pieces + k
        slot = place(side, lax.rem(level + tall - off, tall), k)
        return slot, pltpu.make_async_remote_copy(
            whole.at[slot], whole.at[slot], h_send.at[at], h_recv.at[at],
            device_id={"tensor": sibling}, device_id_type=MESH)

    def products(i):
        fetch(i, sib_side).wait()
        sib_out[i] = jnp.dot(
            head_ref[...], weight[i * 2], preferred_element_type=jnp.float32
        ).astype(jnp.bfloat16)
        to_sibling(i).start()
        fetch(i, core).wait()
        mine = jnp.dot(head_ref[...], weight[i * 2 + 1], preferred_element_type=jnp.float32)
        to_sibling(i).wait_recv()
        return mine + sib_in[i].astype(jnp.float32)

    def far(i, carry):
        y_out[i] = products(i).astype(jnp.bfloat16)
        to_peer(i).start()
        return carry

    lax.fori_loop(0, steps - pieces, far, 0)

    def near(k, carry):
        mixed = products(steps - pieces + k)
        for off in range(1, tall):
            at = (off - 1) * pieces + k
            to_peer(at).wait_recv()
            mixed = mixed + y_in[at].astype(jnp.float32)
        slot = place(core, level, k)
        cols = pl.ds(pl.multiple_of(slot * CHUNK, CHUNK), CHUNK)
        total = resid_ref[:, cols].astype(jnp.float32) + mixed
        whole[slot] = jnp.where(keep_ref[...] > 0.0, total, 0.0).astype(jnp.bfloat16)
        for off in range(1, tall):
            gather_peer(off, k).start()
        hand_over(core, 0, k)[1].start()
        return carry

    lax.fori_loop(0, pieces, near, 0)

    def square(slot):
        wide = whole[slot].astype(jnp.float32)
        return jnp.sum(wide * wide, axis=-1, keepdims=True)

    squares = jnp.zeros((rows, 1), jnp.float32)
    for k in range(pieces):
        squares = squares + square(place(core, level, k))
        slot, copy = hand_over(sib_side, 0, k)
        copy.wait_recv()
        squares = squares + square(slot)
    for k in range(pieces):
        for off in range(1, tall):
            slot, copy = gather_wait(off, k)
            copy.wait_recv()
            hand_over(core, off, k)[1].start()
            squares = squares + square(slot)
    for k in range(pieces):
        for off in range(1, tall):
            slot, copy = hand_over(sib_side, off, k)
            copy.wait_recv()
            squares = squares + square(slot)
    scale = lax.rsqrt(squares * (1.0 / width) + 1e-05)
    for j in range(width // CHUNK):
        cols = pl.ds(j * CHUNK, CHUNK)
        hidden = whole[j]
        hidden_ref[:, cols] = hidden
        normed_ref[:, cols] = (hidden.astype(jnp.float32) * scale * gain_ref[:, cols]).astype(jnp.bfloat16)
    for i in range(steps):
        to_sibling(i).wait_send()
    for i in range(steps - pieces):
        to_peer(i).wait_send()
    for k in range(pieces):
        hand_over(core, 0, k)[1].wait_send()
        for off in range(1, tall):
            gather_peer(off, k).wait_send()
            hand_over(core, off, k)[1].wait_send()


def project(flat_heads, keep_rows, gain, resid_rows, w_out, ranks):
    rows = flat_heads.shape[0]
    depth, width = w_out.shape
    pieces = width // ranks // CHUNK
    steps = ranks // 2 * pieces
    far = steps - pieces
    block = (rows, CHUNK)
    dma = pltpu.SemaphoreType.DMA
    out = jax.ShapeDtypeStruct((rows, width), jnp.bfloat16)
    return pl.pallas_call(
        functools.partial(project_kernel, ranks),
        out_shape=(out, out),
        in_specs=[VMEM, VMEM, VMEM, VMEM, ANY],
        out_specs=(VMEM, VMEM),
        scratch_shapes=[
            pltpu.VMEM((2 * steps, depth, CHUNK), jnp.bfloat16),
            pltpu.VMEM((steps,) + block, jnp.bfloat16),
            pltpu.VMEM((steps,) + block, jnp.bfloat16),
            pltpu.VMEM((far,) + block, jnp.bfloat16),
            pltpu.VMEM((far,) + block, jnp.bfloat16),
            pltpu.VMEM((2 * steps,) + block, jnp.bfloat16),
            dma((2 * steps,)),
            dma((steps,)), dma((steps,)),
            dma((far,)), dma((far,)),
            dma((far,)), dma((far,)),
            dma((steps,)), dma((steps,)),
        ],
        compiler_params=pltpu.CompilerParams(
            collective_id=0, has_side_effects=True, vmem_limit_bytes=56 * 2**20
        ),
        cost_estimate=pl.CostEstimate(
            flops=2 * rows * depth * width, bytes_accessed=2 * depth * width, transcendentals=0
        ),
    )(flat_heads, keep_rows, gain, resid_rows, w_out)


def per_device(ranks, queries, new_kv, pool, lengths, block_table, plan, w_out, residual, norm_gain):
    my_replica = lax.axis_index("replica")
    steps, slots, _ = queries.shape
    head_dim = pool.shape[3] // 2
    copies = pool.shape[2]
    heads = queries.shape[2] // head_dim
    blocks = block_table.shape[1]
    width = w_out.shape[1]
    source_slot, source, target, target_slot = (plan[:, i] for i in range(4))
    order = jnp.arange(plan.shape[0], dtype=jnp.int32)
    slot_ids = jnp.arange(slots, dtype=jnp.int32)
    ranks_of = jnp.arange(SEND, dtype=jnp.int32)
    sending = source == my_replica
    arriving = target == my_replica
    before = order[None, :] < order[:, None]
    position = jnp.sum((source[None, :] == source[:, None]) & before, axis=1)
    selector = sending[None, :] & (position[None, :] == ranks_of[:, None])
    chosen = jnp.sum(jnp.where(selector, source_slot[None, :], 0), axis=1)
    sizes = jnp.sum(jnp.where(slot_ids[None, :] == chosen[:, None], lengths[None, :], 0), axis=1)
    got = lax.all_gather(pack(pool, block_table, chosen, sizes), "replica", axis=0, tiled=True)

    query_rows = queries.reshape(steps, slots, heads, head_dim).transpose(1, 0, 2, 3)
    query_rows = query_rows.reshape(slots, steps * heads, head_dim)
    fresh_rows = new_kv.transpose(1, 0, 2, 3).reshape(slots, steps * copies, 2 * head_dim)
    fresh_rows = jnp.pad(fresh_rows, ((0, 0), (0, 16 - steps * copies), (0, 0)))
    main = attend(query_rows, fresh_rows, pool, block_table, lengths, steps, copies)

    turn = jnp.sum((target[None, :] == target[:, None]) & before, axis=1)
    arrival = arriving[None, :] & (turn[None, :] == ranks_of[:, None])
    from_index = jnp.sum(jnp.where(arrival, (source * SEND + position)[None, :], 0), axis=1)
    to_slot = jnp.sum(jnp.where(arrival, target_slot[None, :], 0), axis=1)
    to_slot = jnp.where(jnp.any(arrival, axis=1), to_slot, -1)
    got_sizes = got[blocks :: blocks + 1, 0, 0, 0].astype(jnp.int32)
    moved_hit = jnp.arange(got_sizes.shape[0], dtype=jnp.int32)[None, :] == from_index[:, None]
    moved_count = jnp.sum(jnp.where(moved_hit, got_sizes[None, :], 0), axis=1)
    moved_table = from_index[:, None] * (blocks + 1) + jnp.arange(blocks, dtype=jnp.int32)[None, :]
    pick = jnp.maximum(to_slot, 0)
    extra = attend(query_rows[pick], fresh_rows[pick], got, moved_table, moved_count, steps, copies)
    head_out = main
    for j in range(SEND):
        head_out = jnp.where((slot_ids == to_slot[j])[:, None, None], extra[j][None], head_out)
    flat_heads = head_out.reshape(slots, steps, heads * head_dim).transpose(1, 0, 2)
    flat_heads = flat_heads.reshape(steps * slots, heads * head_dim)

    incoming = jnp.any(arriving[None, :] & (target_slot[None, :] == slot_ids[:, None]), axis=1)
    moved_out = jnp.any(sending[None, :] & (source_slot[None, :] == slot_ids[:, None]), axis=1)
    live = incoming | (lengths > 0) & jnp.logical_not(moved_out)
    keep_rows = jnp.tile(live, steps)[:, None].astype(jnp.float32)
    gain = norm_gain.astype(jnp.float32)[None, :]
    resid_rows = residual.reshape(steps * slots, width)
    hidden, normed = project(flat_heads, keep_rows, gain, resid_rows, w_out, ranks)
    out_shape = (steps, slots, width)
    return (hidden.reshape(out_shape), normed.reshape(out_shape))


def solution(mesh):
    in_specs = (
        P(None, ("groups", "replica"), "tensor"),
        P(None, ("groups", "replica"), "tensor", None),
        P(("groups", "replica"), None, "tensor", None),
        P(("groups", "replica")),
        P(("groups", "replica"), None),
        P("groups", None),
        P("tensor", None),
        P(None, ("groups", "replica"), None),
        P(),
    )
    out_specs = (P(None, ("groups", "replica"), None), P(None, ("groups", "replica"), None))
    return jax.shard_map(
        functools.partial(per_device, mesh.shape["tensor"]),
        mesh=mesh, in_specs=in_specs, out_specs=out_specs, check_vma=False,
    )
```

```python
import functools
import math

import jax
import jax.numpy as jnp
from jax import lax
from jax.experimental import pallas as pl
from jax.experimental.pallas import tpu as pltpu
from jax.sharding import PartitionSpec as P

SEND = 2
CHUNK = 512
VMEM_ASK = 58 * 2**20
MESH = pl.DeviceIdType.MESH
VMEM = pl.BlockSpec(memory_space=pltpu.VMEM)
ANY = pl.BlockSpec(memory_space=pl.ANY)
SMEM = pl.BlockSpec(memory_space=pltpu.SMEM)


def masks(rows, heads, copies, cached, total):
    row = lax.broadcasted_iota(jnp.int32, (rows, total), 0)
    col = lax.broadcasted_iota(jnp.int32, (rows, total), 1)
    step = row // heads
    copy = (row % heads) // (heads // copies)
    is_fresh = col >= cached
    fresh_step = (col - cached) // copies
    same_copy = (col % copies) == copy
    fresh_ok = is_fresh & same_copy & (fresh_step <= step)
    limit = jnp.where(is_fresh | jnp.logical_not(same_copy), 1 << 20, col)
    return jnp.where(fresh_ok, -1, limit)


def attend_group(queries, keys, values, bounds, limit):
    inv_root = 1.0 / math.sqrt(queries[0].shape[-1])
    scores = [
        lax.dot_general(q, k, (((1,), (1,)), ((), ())), preferred_element_type=jnp.float32)
        for q, k in zip(queries, keys)
    ]
    scores = [jnp.where(limit < c, x * inv_root, -jnp.inf) for x, c in zip(scores, bounds)]
    powers = [jnp.exp(x - jnp.max(x, axis=-1, keepdims=True)) for x in scores]
    weights = [(p * (1.0 / jnp.sum(p, axis=-1, keepdims=True))).astype(jnp.bfloat16) for p in powers]
    return [
        jnp.dot(w, v, preferred_element_type=jnp.float32).astype(jnp.bfloat16) for w, v in zip(weights, values)
    ]


def attend_kernel(dims, table_ref, count_ref, query_ref, fresh_ref, pool_ref, out_ref, keys, values, sems):
    slots, blocks, steps, heads, copies, unroll = dims
    head_dim = query_ref.shape[-1]
    rows = steps * heads
    block_rows = keys.shape[1] * copies
    cached = blocks * block_rows
    get_keys = pltpu.make_async_copy(pool_ref.at[..., pl.ds(0, head_dim)], keys, sems.at[0])
    get_values = pltpu.make_async_copy(pool_ref.at[..., pl.ds(head_dim, head_dim)], values, sems.at[1])
    get_keys.start()
    get_values.start()
    limit = masks(rows, heads, copies, cached, cached + fresh_ref.shape[1])
    get_keys.wait()
    get_values.wait()

    def rows_of(store, new, n):
        found = [store[table_ref[n * blocks + b]].reshape(block_rows, head_dim) for b in range(blocks)]
        return jnp.concatenate(found + [new], axis=0)

    def body(i, carry):
        ids = [i * unroll + u for u in range(unroll)]
        new = [fresh_ref[n] for n in ids]
        got = attend_group(
            [query_ref[n] for n in ids],
            [rows_of(keys, f[:, :head_dim], n) for f, n in zip(new, ids)],
            [rows_of(values, f[:, head_dim:], n) for f, n in zip(new, ids)],
            [count_ref[n] * copies for n in ids],
            limit,
        )
        for n, x in zip(ids, got):
            out_ref[n] = x
        return carry

    lax.fori_loop(0, slots // unroll, body, 0)


def drop_single(pool):
    return pool.reshape(pool.shape[0], pool.shape[1], pool.shape[3]) if pool.shape[2] == 1 else pool


def attend(query_rows, fresh_rows, pool, table, count, steps, copies, unroll):
    slots, rows, head_dim = query_rows.shape
    blocks = table.shape[1]
    dims = (slots, blocks, steps, rows // steps, copies, unroll)
    part = pool.shape[:-1] + (head_dim,)
    return pl.pallas_call(
        functools.partial(attend_kernel, dims),
        out_shape=jax.ShapeDtypeStruct((slots, rows, head_dim), jnp.bfloat16),
        in_specs=[SMEM, SMEM, VMEM, VMEM, ANY],
        out_specs=VMEM,
        scratch_shapes=[
            pltpu.VMEM(part, jnp.bfloat16),
            pltpu.VMEM(part, jnp.bfloat16),
            pltpu.SemaphoreType.DMA((2,)),
        ],
        compiler_params=pltpu.CompilerParams(vmem_limit_bytes=VMEM_ASK),
        cost_estimate=pl.CostEstimate(
            flops=4 * slots * rows * 336 * head_dim, bytes_accessed=4 * pool.size, transcendentals=slots * rows * 336
        ),
    )(table.reshape(-1), count, query_rows, fresh_rows, pool)


def moved_kernel(dims, from_ref, slot_ref, query_ref, fresh_ref, got_ref, main_ref, out_ref):
    blocks, steps, heads, copies = dims
    head_dim = query_ref.shape[-1]
    rows = steps * heads
    cached = blocks * got_ref.shape[1]
    limit = masks(rows, heads, copies, cached, cached + fresh_ref.shape[1])
    out_ref[...] = main_ref[...]
    ids = [jnp.maximum(slot_ref[j], 0) for j in range(SEND)]
    base = [from_ref[j] * (blocks + 1) for j in range(SEND)]

    def rows_of(j, lo):
        found = [got_ref[base[j] + b, :, lo : lo + head_dim] for b in range(blocks)]
        return jnp.concatenate(found + [fresh_ref[ids[j], :, lo : lo + head_dim]], axis=0)

    bounds = [
        got_ref[base[j] + blocks, :, 0:head_dim].astype(jnp.float32)[0:1, 0:1].astype(jnp.int32) * copies
        for j in range(SEND)
    ]
    heads_of = attend_group(
        [query_ref[n] for n in ids],
        [rows_of(j, 0) for j in range(SEND)],
        [rows_of(j, head_dim) for j in range(SEND)],
        bounds,
        limit,
    )
    for j in range(SEND):

        @pl.when(slot_ref[j] >= 0)
        def _():
            out_ref[ids[j]] = heads_of[j]


def attend_moved(query_rows, fresh_rows, got, from_index, to_slot, main, blocks, steps, copies):
    rows = query_rows.shape[1]
    dims = (blocks, steps, rows // steps, copies)
    return pl.pallas_call(
        functools.partial(moved_kernel, dims),
        out_shape=jax.ShapeDtypeStruct(main.shape, main.dtype),
        in_specs=[SMEM, SMEM, VMEM, VMEM, VMEM, VMEM],
        out_specs=VMEM,
    )(from_index, to_slot, query_rows, fresh_rows, got, main)


def pack_kernel(blocks, head_dim, table_ref, chosen_ref, size_ref, pool_ref, out_ref, keys, values, sems):
    copies = []
    for j in range(SEND):
        for b in range(blocks):
            at = j * blocks + b
            block = pool_ref.at[table_ref[chosen_ref[j] * blocks + b]]
            for half, store in enumerate((keys, values)):
                part = block.at[..., pl.ds(half * head_dim, head_dim)]
                copies.append(pltpu.make_async_copy(part, store.at[at], sems.at[2 * at + half]))
                copies[-1].start()
    shape = out_ref.shape[1:]
    for j in range(SEND):
        size = jnp.full(shape, size_ref[j], jnp.int32)
        out_ref[j * (blocks + 1) + blocks] = size.astype(jnp.float32).astype(jnp.bfloat16)
    for copy in copies:
        copy.wait()
    for j in range(SEND):
        for b in range(blocks):
            for half, store in enumerate((keys, values)):
                cols = pl.ds(half * head_dim, head_dim)
                out_ref[j * (blocks + 1) + b, :, cols] = store[j * blocks + b].reshape(shape[0], head_dim)


def pack(pool, table, chosen, sizes, copies):
    blocks = table.shape[1]
    head_dim = pool.shape[-1] // 2
    part = pool.shape[1:-1] + (head_dim,)
    shape = (SEND * (blocks + 1), pool.shape[1] * copies, 2 * head_dim)
    return pl.pallas_call(
        functools.partial(pack_kernel, blocks, head_dim),
        out_shape=jax.ShapeDtypeStruct(shape, pool.dtype),
        in_specs=[SMEM, SMEM, SMEM, ANY],
        out_specs=VMEM,
        scratch_shapes=[
            pltpu.VMEM((SEND * blocks,) + part, pool.dtype),
            pltpu.VMEM((SEND * blocks,) + part, pool.dtype),
            pltpu.SemaphoreType.DMA((2 * SEND * blocks,)),
        ],
        compiler_params=pltpu.CompilerParams(vmem_limit_bytes=VMEM_ASK),
    )(table.reshape(-1), chosen, sizes, pool)


def project_kernel(ranks, head_ref, keep_ref, resid_ref, w_ref, hidden_ref, scale_ref,
                   weight, sib_out, sib_in, y_out, y_in, whole, w_sem, s_send, s_recv, y_send, y_recv,
                   g_send, g_recv, h_send, h_recv):
    rows, width = hidden_ref.shape
    tall = ranks // 2
    pieces = width // ranks // CHUNK
    me = lax.axis_index("tensor")
    level = me // 2
    core = me % 2
    sibling = level * 2 + 1 - core

    def place(side, at_level, k):
        return (side * tall + at_level) * pieces + k

    def peer(off):
        return lax.rem(level + off, tall) * 2 + core

    barrier = pltpu.get_barrier_semaphore()
    pl.semaphore_signal(barrier, inc=1, device_id={"tensor": sibling}, device_id_type=MESH)
    for off in range(1, tall):
        pl.semaphore_signal(barrier, inc=1, device_id={"tensor": peer(off)}, device_id_type=MESH)

    def fetch(i, side):
        at_level = lax.rem(level + 1 + i // pieces, tall)
        chunk = place(side, at_level, lax.rem(i, pieces))
        slot = i * 2 + (0 if side is sib_side else 1)
        return pltpu.make_async_copy(
            w_ref.at[:, pl.ds(pl.multiple_of(chunk * CHUNK, CHUNK), CHUNK)], weight.at[slot], w_sem.at[slot]
        )

    sib_side = 1 - core
    steps = tall * pieces

    def start_fetch(i, carry):
        fetch(i, sib_side).start()
        fetch(i, core).start()
        return carry

    lax.fori_loop(0, steps, start_fetch, 0)
    pl.semaphore_wait(barrier, tall)

    def to_sibling(i):
        return pltpu.make_async_remote_copy(
            sib_out.at[i], sib_in.at[i], s_send.at[i], s_recv.at[i],
            device_id={"tensor": sibling}, device_id_type=MESH)

    def to_peer(i):
        off = 1 + i // pieces
        return pltpu.make_async_remote_copy(
            y_out.at[i], y_in.at[i], y_send.at[i], y_recv.at[i],
            device_id={"tensor": peer(off)}, device_id_type=MESH)

    def gather_peer(off, k):
        at = (off - 1) * pieces + k
        slot = place(core, level, k)
        return pltpu.make_async_remote_copy(
            whole.at[slot], whole.at[slot], g_send.at[at], g_recv.at[at],
            device_id={"tensor": peer(off)}, device_id_type=MESH)

    def gather_wait(off, k):
        at = (off - 1) * pieces + k
        slot = place(core, lax.rem(level + tall - off, tall), k)
        return slot, pltpu.make_async_remote_copy(
            whole.at[slot], whole.at[slot], g_send.at[at], g_recv.at[at],
            device_id={"tensor": peer(off)}, device_id_type=MESH)

    def hand_over(side, off, k):
        at = off * pieces + k
        slot = place(side, lax.rem(level + tall - off, tall), k)
        return slot, pltpu.make_async_remote_copy(
            whole.at[slot], whole.at[slot], h_send.at[at], h_recv.at[at],
            device_id={"tensor": sibling}, device_id_type=MESH)

    def products(i):
        fetch(i, sib_side).wait()
        sib_out[i] = jnp.dot(
            head_ref[...], weight[i * 2], preferred_element_type=jnp.float32
        ).astype(jnp.bfloat16)
        to_sibling(i).start()
        fetch(i, core).wait()
        mine = jnp.dot(head_ref[...], weight[i * 2 + 1], preferred_element_type=jnp.float32)
        to_sibling(i).wait_recv()
        return mine + sib_in[i].astype(jnp.float32)

    def far(i, carry):
        y_out[i] = products(i).astype(jnp.bfloat16)
        to_peer(i).start()
        return carry

    lax.fori_loop(0, steps - pieces, far, 0)

    def near(k, carry):
        mixed = products(steps - pieces + k)
        for off in range(1, tall):
            at = (off - 1) * pieces + k
            to_peer(at).wait_recv()
            mixed = mixed + y_in[at].astype(jnp.float32)
        slot = place(core, level, k)
        cols = pl.ds(pl.multiple_of(slot * CHUNK, CHUNK), CHUNK)
        total = resid_ref[:, cols].astype(jnp.float32) + mixed
        whole[slot] = jnp.where(keep_ref[...] > 0.0, total, 0.0).astype(jnp.bfloat16)
        for off in range(1, tall):
            gather_peer(off, k).start()
        hand_over(core, 0, k)[1].start()
        return carry

    lax.fori_loop(0, pieces, near, 0)

    def square(slot):
        wide = whole[slot].astype(jnp.float32)
        return jnp.sum(wide * wide, axis=-1, keepdims=True)

    squares = jnp.zeros((rows, 1), jnp.float32)
    for k in range(pieces):
        squares = squares + square(place(core, level, k))
        slot, copy = hand_over(sib_side, 0, k)
        copy.wait_recv()
        squares = squares + square(slot)
    for k in range(pieces):
        for off in range(1, tall):
            slot, copy = gather_wait(off, k)
            copy.wait_recv()
            hand_over(core, off, k)[1].start()
            squares = squares + square(slot)
    for k in range(pieces):
        for off in range(1, tall):
            slot, copy = hand_over(sib_side, off, k)
            copy.wait_recv()
            squares = squares + square(slot)
    scale_ref[...] = lax.rsqrt(squares * (1.0 / width) + 1e-05)
    for j in range(width // CHUNK):
        hidden_ref[:, pl.ds(j * CHUNK, CHUNK)] = whole[j]
    for i in range(steps):
        to_sibling(i).wait_send()
    for i in range(steps - pieces):
        to_peer(i).wait_send()
    for k in range(pieces):
        hand_over(core, 0, k)[1].wait_send()
        for off in range(1, tall):
            gather_peer(off, k).wait_send()
            hand_over(core, off, k)[1].wait_send()


def project(flat_heads, keep_rows, resid_rows, w_out, ranks):
    rows = flat_heads.shape[0]
    depth, width = w_out.shape
    pieces = width // ranks // CHUNK
    steps = ranks // 2 * pieces
    far = steps - pieces
    block = (rows, CHUNK)
    dma = pltpu.SemaphoreType.DMA
    out = jax.ShapeDtypeStruct((rows, width), jnp.bfloat16)
    return pl.pallas_call(
        functools.partial(project_kernel, ranks),
        out_shape=(out, jax.ShapeDtypeStruct((rows, 1), jnp.float32)),
        in_specs=[VMEM, VMEM, VMEM, ANY],
        out_specs=(VMEM, VMEM),
        scratch_shapes=[
            pltpu.VMEM((2 * steps, depth, CHUNK), jnp.bfloat16),
            pltpu.VMEM((steps,) + block, jnp.bfloat16),
            pltpu.VMEM((steps,) + block, jnp.bfloat16),
            pltpu.VMEM((far,) + block, jnp.bfloat16),
            pltpu.VMEM((far,) + block, jnp.bfloat16),
            pltpu.VMEM((2 * steps,) + block, jnp.bfloat16),
            dma((2 * steps,)),
            dma((steps,)), dma((steps,)),
            dma((far,)), dma((far,)),
            dma((far,)), dma((far,)),
            dma((steps,)), dma((steps,)),
        ],
        compiler_params=pltpu.CompilerParams(
            collective_id=0, has_side_effects=True, vmem_limit_bytes=56 * 2**20
        ),
        cost_estimate=pl.CostEstimate(
            flops=2 * rows * depth * width, bytes_accessed=2 * depth * width, transcendentals=0
        ),
    )(flat_heads, keep_rows, resid_rows, w_out)


def per_device(ranks, queries, new_kv, pool, lengths, block_table, plan, w_out, residual, norm_gain):
    my_replica = lax.axis_index("replica")
    steps, slots, _ = queries.shape
    head_dim = pool.shape[3] // 2
    copies = pool.shape[2]
    heads = queries.shape[2] // head_dim
    blocks = block_table.shape[1]
    width = w_out.shape[1]
    source_slot, source, target, target_slot = (plan[:, i] for i in range(4))
    order = jnp.arange(plan.shape[0], dtype=jnp.int32)
    slot_ids = jnp.arange(slots, dtype=jnp.int32)
    ranks_of = jnp.arange(SEND, dtype=jnp.int32)
    sending = source == my_replica
    arriving = target == my_replica
    before = order[None, :] < order[:, None]
    position = jnp.sum((source[None, :] == source[:, None]) & before, axis=1)
    selector = sending[None, :] & (position[None, :] == ranks_of[:, None])
    chosen = jnp.sum(jnp.where(selector, source_slot[None, :], 0), axis=1)
    sizes = jnp.sum(jnp.where(slot_ids[None, :] == chosen[:, None], lengths[None, :], 0), axis=1)
    pool = drop_single(pool)
    got = lax.all_gather(pack(pool, block_table, chosen, sizes, copies), "replica", axis=0, tiled=True)

    query_rows = queries.reshape(steps, slots, heads, head_dim).transpose(1, 0, 2, 3)
    query_rows = query_rows.reshape(slots, steps * heads, head_dim)
    fresh_rows = new_kv.transpose(1, 0, 2, 3).reshape(slots, steps * copies, 2 * head_dim)
    fresh_rows = jnp.pad(fresh_rows, ((0, 0), (0, 16 - steps * copies), (0, 0)))
    main = attend(query_rows, fresh_rows, pool, block_table, lengths, steps, copies, 8)

    turn = jnp.sum((target[None, :] == target[:, None]) & before, axis=1)
    arrival = arriving[None, :] & (turn[None, :] == ranks_of[:, None])
    from_index = jnp.sum(jnp.where(arrival, (source * SEND + position)[None, :], 0), axis=1)
    to_slot = jnp.sum(jnp.where(arrival, target_slot[None, :], 0), axis=1)
    to_slot = jnp.where(jnp.any(arrival, axis=1), to_slot, -1)
    head_out = attend_moved(query_rows, fresh_rows, got, from_index, to_slot, main, blocks, steps, copies)
    flat_heads = head_out.reshape(slots, steps, heads * head_dim).transpose(1, 0, 2)
    flat_heads = flat_heads.reshape(steps * slots, heads * head_dim)

    incoming = jnp.any(arriving[None, :] & (target_slot[None, :] == slot_ids[:, None]), axis=1)
    moved_out = jnp.any(sending[None, :] & (source_slot[None, :] == slot_ids[:, None]), axis=1)
    live = incoming | (lengths > 0) & jnp.logical_not(moved_out)
    keep_rows = jnp.tile(live, steps)[:, None].astype(jnp.float32)
    resid_rows = residual.reshape(steps * slots, width)
    hidden, scale = project(flat_heads, keep_rows, resid_rows, w_out, ranks)
    gain = norm_gain.astype(jnp.float32)[None, :]
    normed = (hidden.astype(jnp.float32) * scale * gain).astype(jnp.bfloat16)
    out_shape = (steps, slots, width)
    return (hidden.reshape(out_shape), normed.reshape(out_shape))


def solution(mesh):
    in_specs = (
        P(None, ("groups", "replica"), "tensor"),
        P(None, ("groups", "replica"), "tensor", None),
        P(("groups", "replica"), None, "tensor", None),
        P(("groups", "replica")),
        P(("groups", "replica"), None),
        P("groups", None),
        P("tensor", None),
        P(None, ("groups", "replica"), None),
        P(),
    )
    out_specs = (P(None, ("groups", "replica"), None), P(None, ("groups", "replica"), None))
    return jax.shard_map(
        functools.partial(per_device, mesh.shape["tensor"]),
        mesh=mesh, in_specs=in_specs, out_specs=out_specs, check_vma=False,
    )
```

```python
import functools
import math

import jax
import jax.numpy as jnp
from jax import lax
from jax.experimental import pallas as pl
from jax.experimental.pallas import tpu as pltpu
from jax.sharding import PartitionSpec as P

CHUNK = 512
VMEM_ASK = 58 * 2**20
MESH = pl.DeviceIdType.MESH
VMEM = pl.BlockSpec(memory_space=pltpu.VMEM)
ANY = pl.BlockSpec(memory_space=pl.ANY)
SMEM = pl.BlockSpec(memory_space=pltpu.SMEM)


def masks(rows, heads, copies, cached, total):
    row = lax.broadcasted_iota(jnp.int32, (rows, total), 0)
    col = lax.broadcasted_iota(jnp.int32, (rows, total), 1)
    step = row // heads
    copy = (row % heads) // (heads // copies)
    is_fresh = col >= cached
    fresh_step = (col - cached) // copies
    same_copy = (col % copies) == copy
    fresh_ok = is_fresh & same_copy & (fresh_step <= step)
    limit = jnp.where(is_fresh | jnp.logical_not(same_copy), 1 << 20, col)
    return jnp.where(fresh_ok, -1, limit)


def attend_group(queries, keys, values, bounds, limit):
    inv_root = 1.0 / math.sqrt(queries[0].shape[-1])
    scores = [
        lax.dot_general(q, k, (((1,), (1,)), ((), ())), preferred_element_type=jnp.float32)
        for q, k in zip(queries, keys)
    ]
    scores = [jnp.where(limit < c, x * inv_root, -jnp.inf) for x, c in zip(scores, bounds)]
    powers = [jnp.exp(x - jnp.max(x, axis=-1, keepdims=True)) for x in scores]
    weights = [(p * (1.0 / jnp.sum(p, axis=-1, keepdims=True))).astype(jnp.bfloat16) for p in powers]
    return [
        jnp.dot(w, v, preferred_element_type=jnp.float32).astype(jnp.bfloat16) for w, v in zip(weights, values)
    ]


def attend_kernel(dims, table_ref, count_ref, query_ref, fresh_ref, pool_ref, out_ref, keys, values, sems):
    slots, blocks, steps, heads, copies, unroll = dims
    head_dim = query_ref.shape[-1]
    rows = steps * heads
    block_rows = keys.shape[1] * copies
    cached = blocks * block_rows
    get_keys = pltpu.make_async_copy(pool_ref.at[..., pl.ds(0, head_dim)], keys, sems.at[0])
    get_values = pltpu.make_async_copy(pool_ref.at[..., pl.ds(head_dim, head_dim)], values, sems.at[1])
    get_keys.start()
    get_values.start()
    limit = masks(rows, heads, copies, cached, cached + fresh_ref.shape[1])
    get_keys.wait()
    get_values.wait()

    def rows_of(store, new, n):
        found = [store[table_ref[n * blocks + b]].reshape(block_rows, head_dim) for b in range(blocks)]
        return jnp.concatenate(found + [new], axis=0)

    def body(i, carry):
        ids = [i * unroll + u for u in range(unroll)]
        new = [fresh_ref[n] for n in ids]
        got = attend_group(
            [query_ref[n] for n in ids],
            [rows_of(keys, f[:, :head_dim], n) for f, n in zip(new, ids)],
            [rows_of(values, f[:, head_dim:], n) for f, n in zip(new, ids)],
            [count_ref[n] * copies for n in ids],
            limit,
        )
        for n, x in zip(ids, got):
            out_ref[n] = x
        return carry

    lax.fori_loop(0, slots // unroll, body, 0)


def drop_single(pool):
    return pool.reshape(pool.shape[0], pool.shape[1], pool.shape[3]) if pool.shape[2] == 1 else pool


def attend(query_rows, fresh_rows, pool, table, count, steps, copies, unroll):
    slots, rows, head_dim = query_rows.shape
    blocks = table.shape[1]
    dims = (slots, blocks, steps, rows // steps, copies, unroll)
    part = pool.shape[:-1] + (head_dim,)
    return pl.pallas_call(
        functools.partial(attend_kernel, dims),
        out_shape=jax.ShapeDtypeStruct((slots, rows, head_dim), jnp.bfloat16),
        in_specs=[SMEM, SMEM, VMEM, VMEM, ANY],
        out_specs=VMEM,
        scratch_shapes=[
            pltpu.VMEM(part, jnp.bfloat16),
            pltpu.VMEM(part, jnp.bfloat16),
            pltpu.SemaphoreType.DMA((2,)),
        ],
        compiler_params=pltpu.CompilerParams(vmem_limit_bytes=VMEM_ASK),
        cost_estimate=pl.CostEstimate(
            flops=4 * slots * rows * 336 * head_dim, bytes_accessed=4 * pool.size, transcendentals=slots * rows * 336
        ),
    )(table.reshape(-1), count, query_rows, fresh_rows, pool)


def moved_kernel(dims, slot_ref, query_ref, fresh_ref, main_ref, *refs):
    blocks, steps, heads, copies = dims
    got_refs, out_ref = refs[:-1], refs[-1]
    moves = range(len(got_refs))
    head_dim = query_ref.shape[-1]
    rows = steps * heads
    cached = blocks * got_refs[0].shape[1]
    limit = masks(rows, heads, copies, cached, cached + fresh_ref.shape[1])
    out_ref[...] = main_ref[...]
    ids = [jnp.maximum(slot_ref[j], 0) for j in moves]

    def rows_of(j, lo):
        found = [got_refs[j][b, :, lo : lo + head_dim] for b in range(blocks)]
        return jnp.concatenate(found + [fresh_ref[ids[j], :, lo : lo + head_dim]], axis=0)

    bounds = [
        got_refs[j][blocks, :, 0:head_dim].astype(jnp.float32)[0:1, 0:1].astype(jnp.int32) * copies
        for j in moves
    ]
    heads_of = attend_group(
        [query_ref[n] for n in ids],
        [rows_of(j, 0) for j in moves],
        [rows_of(j, head_dim) for j in moves],
        bounds,
        limit,
    )
    for j in moves:

        @pl.when(slot_ref[j] >= 0)
        def _():
            out_ref[ids[j]] = heads_of[j]


def attend_moved(query_rows, fresh_rows, got, to_slot, main, blocks, steps, copies):
    rows = query_rows.shape[1]
    dims = (blocks, steps, rows // steps, copies)
    return pl.pallas_call(
        functools.partial(moved_kernel, dims),
        out_shape=jax.ShapeDtypeStruct(main.shape, main.dtype),
        in_specs=[SMEM, VMEM, VMEM, VMEM] + [VMEM] * len(got),
        out_specs=VMEM,
    )(to_slot, query_rows, fresh_rows, main, *got)


def pack_kernel(blocks, head_dim, table_ref, chosen_ref, size_ref, pool_ref, *refs):
    out_refs, (keys, values, sems) = refs[:-3], refs[-3:]
    copies = []
    for j in range(len(out_refs)):
        for b in range(blocks):
            at = j * blocks + b
            block = pool_ref.at[table_ref[chosen_ref[j] * blocks + b]]
            for half, store in enumerate((keys, values)):
                part = block.at[..., pl.ds(half * head_dim, head_dim)]
                copies.append(pltpu.make_async_copy(part, store.at[at], sems.at[2 * at + half]))
                copies[-1].start()
    shape = out_refs[0].shape[1:]
    for j, out_ref in enumerate(out_refs):
        size = jnp.full(shape, size_ref[j], jnp.int32)
        out_ref[blocks] = size.astype(jnp.float32).astype(jnp.bfloat16)
    for copy in copies:
        copy.wait()
    for j, out_ref in enumerate(out_refs):
        for b in range(blocks):
            for half, store in enumerate((keys, values)):
                cols = pl.ds(half * head_dim, head_dim)
                out_ref[b, :, cols] = store[j * blocks + b].reshape(shape[0], head_dim)


def pack(pool, table, chosen, sizes, copies):
    blocks = table.shape[1]
    moves = chosen.shape[0]
    head_dim = pool.shape[-1] // 2
    part = (moves * blocks,) + pool.shape[1:-1] + (head_dim,)
    out = jax.ShapeDtypeStruct((blocks + 1, pool.shape[1] * copies, 2 * head_dim), pool.dtype)
    return pl.pallas_call(
        functools.partial(pack_kernel, blocks, head_dim),
        out_shape=(out,) * moves,
        in_specs=[SMEM, SMEM, SMEM, ANY],
        out_specs=(VMEM,) * moves,
        scratch_shapes=[
            pltpu.VMEM(part, pool.dtype),
            pltpu.VMEM(part, pool.dtype),
            pltpu.SemaphoreType.DMA((2 * moves * blocks,)),
        ],
        compiler_params=pltpu.CompilerParams(vmem_limit_bytes=VMEM_ASK),
    )(table.reshape(-1), chosen, sizes, pool)


def project_kernel(ranks, head_ref, keep_ref, resid_ref, w_ref, hidden_ref, scale_ref,
                   weight, sib_out, sib_in, y_out, y_in, whole, w_sem, s_send, s_recv, y_send, y_recv,
                   g_send, g_recv, h_send, h_recv):
    rows, width = hidden_ref.shape
    tall = ranks // 2
    pieces = width // ranks // CHUNK
    me = lax.axis_index("tensor")
    level = me // 2
    core = me % 2
    sibling = level * 2 + 1 - core

    def place(side, at_level, k):
        return (side * tall + at_level) * pieces + k

    def peer(off):
        return lax.rem(level + off, tall) * 2 + core

    barrier = pltpu.get_barrier_semaphore()
    pl.semaphore_signal(barrier, inc=1, device_id={"tensor": sibling}, device_id_type=MESH)
    for off in range(1, tall):
        pl.semaphore_signal(barrier, inc=1, device_id={"tensor": peer(off)}, device_id_type=MESH)

    def fetch(i, side):
        at_level = lax.rem(level + 1 + i // pieces, tall)
        chunk = place(side, at_level, lax.rem(i, pieces))
        slot = i * 2 + (0 if side is sib_side else 1)
        return pltpu.make_async_copy(
            w_ref.at[:, pl.ds(pl.multiple_of(chunk * CHUNK, CHUNK), CHUNK)], weight.at[slot], w_sem.at[slot]
        )

    sib_side = 1 - core
    steps = tall * pieces

    def start_fetch(i, carry):
        fetch(i, sib_side).start()
        fetch(i, core).start()
        return carry

    lax.fori_loop(0, steps, start_fetch, 0)
    pl.semaphore_wait(barrier, tall)

    def to_sibling(i):
        return pltpu.make_async_remote_copy(
            sib_out.at[i], sib_in.at[i], s_send.at[i], s_recv.at[i],
            device_id={"tensor": sibling}, device_id_type=MESH)

    def to_peer(i):
        off = 1 + i // pieces
        return pltpu.make_async_remote_copy(
            y_out.at[i], y_in.at[i], y_send.at[i], y_recv.at[i],
            device_id={"tensor": peer(off)}, device_id_type=MESH)

    def gather_peer(off, k):
        at = (off - 1) * pieces + k
        slot = place(core, level, k)
        return pltpu.make_async_remote_copy(
            whole.at[slot], whole.at[slot], g_send.at[at], g_recv.at[at],
            device_id={"tensor": peer(off)}, device_id_type=MESH)

    def gather_wait(off, k):
        at = (off - 1) * pieces + k
        slot = place(core, lax.rem(level + tall - off, tall), k)
        return slot, pltpu.make_async_remote_copy(
            whole.at[slot], whole.at[slot], g_send.at[at], g_recv.at[at],
            device_id={"tensor": peer(off)}, device_id_type=MESH)

    def hand_over(side, off, k):
        at = off * pieces + k
        slot = place(side, lax.rem(level + tall - off, tall), k)
        return slot, pltpu.make_async_remote_copy(
            whole.at[slot], whole.at[slot], h_send.at[at], h_recv.at[at],
            device_id={"tensor": sibling}, device_id_type=MESH)

    def products(i):
        fetch(i, sib_side).wait()
        sib_out[i] = jnp.dot(
            head_ref[...], weight[i * 2], preferred_element_type=jnp.float32
        ).astype(jnp.bfloat16)
        to_sibling(i).start()
        fetch(i, core).wait()
        mine = jnp.dot(head_ref[...], weight[i * 2 + 1], preferred_element_type=jnp.float32)
        to_sibling(i).wait_recv()
        return mine + sib_in[i].astype(jnp.float32)

    def far(i, carry):
        y_out[i] = products(i).astype(jnp.bfloat16)
        to_peer(i).start()
        return carry

    lax.fori_loop(0, steps - pieces, far, 0)

    def near(k, carry):
        mixed = products(steps - pieces + k)
        for off in range(1, tall):
            at = (off - 1) * pieces + k
            to_peer(at).wait_recv()
            mixed = mixed + y_in[at].astype(jnp.float32)
        slot = place(core, level, k)
        cols = pl.ds(pl.multiple_of(slot * CHUNK, CHUNK), CHUNK)
        total = resid_ref[:, cols].astype(jnp.float32) + mixed
        whole[slot] = jnp.where(keep_ref[...] > 0.0, total, 0.0).astype(jnp.bfloat16)
        for off in range(1, tall):
            gather_peer(off, k).start()
        hand_over(core, 0, k)[1].start()
        return carry

    lax.fori_loop(0, pieces, near, 0)

    def square(slot):
        wide = whole[slot].astype(jnp.float32)
        return jnp.sum(wide * wide, axis=-1, keepdims=True)

    squares = jnp.zeros((rows, 1), jnp.float32)
    for k in range(pieces):
        squares = squares + square(place(core, level, k))
        slot, copy = hand_over(sib_side, 0, k)
        copy.wait_recv()
        squares = squares + square(slot)
    for k in range(pieces):
        for off in range(1, tall):
            slot, copy = gather_wait(off, k)
            copy.wait_recv()
            hand_over(core, off, k)[1].start()
            squares = squares + square(slot)
    for k in range(pieces):
        for off in range(1, tall):
            slot, copy = hand_over(sib_side, off, k)
            copy.wait_recv()
            squares = squares + square(slot)
    scale_ref[...] = lax.rsqrt(squares * (1.0 / width) + 1e-05)
    for j in range(width // CHUNK):
        hidden_ref[:, pl.ds(j * CHUNK, CHUNK)] = whole[j]
    for i in range(steps):
        to_sibling(i).wait_send()
    for i in range(steps - pieces):
        to_peer(i).wait_send()
    for k in range(pieces):
        hand_over(core, 0, k)[1].wait_send()
        for off in range(1, tall):
            gather_peer(off, k).wait_send()
            hand_over(core, off, k)[1].wait_send()


def project(flat_heads, keep_rows, resid_rows, w_out, ranks):
    rows = flat_heads.shape[0]
    depth, width = w_out.shape
    pieces = width // ranks // CHUNK
    steps = ranks // 2 * pieces
    far = steps - pieces
    block = (rows, CHUNK)
    dma = pltpu.SemaphoreType.DMA
    out = jax.ShapeDtypeStruct((rows, width), jnp.bfloat16)
    return pl.pallas_call(
        functools.partial(project_kernel, ranks),
        out_shape=(out, jax.ShapeDtypeStruct((rows, 1), jnp.float32)),
        in_specs=[VMEM, VMEM, VMEM, ANY],
        out_specs=(VMEM, VMEM),
        scratch_shapes=[
            pltpu.VMEM((2 * steps, depth, CHUNK), jnp.bfloat16),
            pltpu.VMEM((steps,) + block, jnp.bfloat16),
            pltpu.VMEM((steps,) + block, jnp.bfloat16),
            pltpu.VMEM((far,) + block, jnp.bfloat16),
            pltpu.VMEM((far,) + block, jnp.bfloat16),
            pltpu.VMEM((2 * steps,) + block, jnp.bfloat16),
            dma((2 * steps,)),
            dma((steps,)), dma((steps,)),
            dma((far,)), dma((far,)),
            dma((far,)), dma((far,)),
            dma((steps,)), dma((steps,)),
        ],
        compiler_params=pltpu.CompilerParams(
            collective_id=0, has_side_effects=True, vmem_limit_bytes=56 * 2**20
        ),
        cost_estimate=pl.CostEstimate(
            flops=2 * rows * depth * width, bytes_accessed=2 * depth * width, transcendentals=0
        ),
    )(flat_heads, keep_rows, resid_rows, w_out)


def per_device(replicas, ranks, queries, new_kv, pool, lengths, block_table, plan, w_out, residual, norm_gain):
    my_replica = lax.axis_index("replica")
    steps, slots, _ = queries.shape
    head_dim = pool.shape[3] // 2
    copies = pool.shape[2]
    heads = queries.shape[2] // head_dim
    blocks = block_table.shape[1]
    width = w_out.shape[1]
    source_slot, source, target, target_slot = (plan[:, i] for i in range(4))
    slot_ids = jnp.arange(slots, dtype=jnp.int32)
    sending = source == my_replica
    arriving = target == my_replica
    shifts = jnp.arange(1, replicas, dtype=jnp.int32)
    leaving = sending[None, :] & (target[None, :] == ((my_replica + shifts) % replicas)[:, None])
    chosen = jnp.sum(jnp.where(leaving, source_slot[None, :], 0), axis=1)
    sizes = jnp.sum(jnp.where(slot_ids[None, :] == chosen[:, None], lengths[None, :], 0), axis=1)
    pool = drop_single(pool)
    got = [
        lax.ppermute(block, "replica", [(r, (r + d) % replicas) for r in range(replicas)])
        for d, block in enumerate(pack(pool, block_table, chosen, sizes, copies), 1)
    ]

    query_rows = queries.reshape(steps, slots, heads, head_dim).transpose(1, 0, 2, 3)
    query_rows = query_rows.reshape(slots, steps * heads, head_dim)
    fresh_rows = new_kv.transpose(1, 0, 2, 3).reshape(slots, steps * copies, 2 * head_dim)
    fresh_rows = jnp.pad(fresh_rows, ((0, 0), (0, 16 - steps * copies), (0, 0)))
    main = attend(query_rows, fresh_rows, pool, block_table, lengths, steps, copies, 8)

    arrival = arriving[None, :] & (source[None, :] == ((my_replica - shifts) % replicas)[:, None])
    to_slot = jnp.sum(jnp.where(arrival, target_slot[None, :] + 1, 0), axis=1) - 1
    head_out = attend_moved(query_rows, fresh_rows, got, to_slot, main, blocks, steps, copies)
    flat_heads = head_out.reshape(slots, steps, heads * head_dim).transpose(1, 0, 2)
    flat_heads = flat_heads.reshape(steps * slots, heads * head_dim)

    incoming = jnp.any(arriving[None, :] & (target_slot[None, :] == slot_ids[:, None]), axis=1)
    moved_out = jnp.any(sending[None, :] & (source_slot[None, :] == slot_ids[:, None]), axis=1)
    live = incoming | (lengths > 0) & jnp.logical_not(moved_out)
    keep_rows = jnp.tile(live, steps)[:, None].astype(jnp.float32)
    resid_rows = residual.reshape(steps * slots, width)
    hidden, scale = project(flat_heads, keep_rows, resid_rows, w_out, ranks)
    gain = norm_gain.astype(jnp.float32)[None, :]
    normed = (hidden.astype(jnp.float32) * scale * gain).astype(jnp.bfloat16)
    out_shape = (steps, slots, width)
    return (hidden.reshape(out_shape), normed.reshape(out_shape))


def solution(mesh):
    in_specs = (
        P(None, ("groups", "replica"), "tensor"),
        P(None, ("groups", "replica"), "tensor", None),
        P(("groups", "replica"), None, "tensor", None),
        P(("groups", "replica")),
        P(("groups", "replica"), None),
        P("groups", None),
        P("tensor", None),
        P(None, ("groups", "replica"), None),
        P(),
    )
    out_specs = (P(None, ("groups", "replica"), None), P(None, ("groups", "replica"), None))
    return jax.shard_map(
        functools.partial(per_device, mesh.shape["replica"], mesh.shape["tensor"]),
        mesh=mesh, in_specs=in_specs, out_specs=out_specs, check_vma=False,
    )
```

```python
import functools
import math

import jax
import jax.numpy as jnp
from jax import lax
from jax.experimental import pallas as pl
from jax.experimental.pallas import tpu as pltpu
from jax.sharding import PartitionSpec as P

CHUNK = 512
VMEM_ASK = 58 * 2**20
MESH = pl.DeviceIdType.MESH
VMEM = pl.BlockSpec(memory_space=pltpu.VMEM)
ANY = pl.BlockSpec(memory_space=pl.ANY)
SMEM = pl.BlockSpec(memory_space=pltpu.SMEM)


def masks(rows, heads, copies, cached, total):
    row = lax.broadcasted_iota(jnp.int32, (rows, total), 0)
    col = lax.broadcasted_iota(jnp.int32, (rows, total), 1)
    step = row // heads
    copy = (row % heads) // (heads // copies)
    is_fresh = col >= cached
    fresh_step = (col - cached) // copies
    same_copy = (col % copies) == copy
    fresh_ok = is_fresh & same_copy & (fresh_step <= step)
    limit = jnp.where(is_fresh | jnp.logical_not(same_copy), 1 << 20, col)
    return jnp.where(fresh_ok, -1, limit)


def attend_group(queries, keys, values, bounds, limit):
    inv_root = 1.0 / math.sqrt(queries[0].shape[-1])
    scores = [
        lax.dot_general(q, k, (((1,), (1,)), ((), ())), preferred_element_type=jnp.float32)
        for q, k in zip(queries, keys)
    ]
    scores = [jnp.where(limit < c, x * inv_root, -jnp.inf) for x, c in zip(scores, bounds)]
    powers = [jnp.exp(x - jnp.max(x, axis=-1, keepdims=True)) for x in scores]
    weights = [(p * (1.0 / jnp.sum(p, axis=-1, keepdims=True))).astype(jnp.bfloat16) for p in powers]
    return [
        jnp.dot(w, v, preferred_element_type=jnp.float32).astype(jnp.bfloat16) for w, v in zip(weights, values)
    ]


def attend_kernel(dims, table_ref, count_ref, query_ref, fresh_ref, pool_ref, out_ref, keys, values, sems):
    slots, blocks, steps, heads, copies, unroll = dims
    head_dim = query_ref.shape[-1]
    rows = steps * heads
    block_rows = keys.shape[1] * copies
    cached = blocks * block_rows
    get_keys = pltpu.make_async_copy(pool_ref.at[..., pl.ds(0, head_dim)], keys, sems.at[0])
    get_values = pltpu.make_async_copy(pool_ref.at[..., pl.ds(head_dim, head_dim)], values, sems.at[1])
    get_keys.start()
    get_values.start()
    limit = masks(rows, heads, copies, cached, cached + fresh_ref.shape[1])
    get_keys.wait()
    get_values.wait()

    def rows_of(store, new, n):
        found = [store[table_ref[n, b]].reshape(block_rows, head_dim) for b in range(blocks)]
        return jnp.concatenate(found + [new], axis=0)

    def body(i, carry):
        ids = [i * unroll + u for u in range(unroll)]
        new = [fresh_ref[n] for n in ids]
        got = attend_group(
            [query_ref[n] for n in ids],
            [rows_of(keys, f[:, :head_dim], n) for f, n in zip(new, ids)],
            [rows_of(values, f[:, head_dim:], n) for f, n in zip(new, ids)],
            [count_ref[n] * copies for n in ids],
            limit,
        )
        for n, x in zip(ids, got):
            out_ref[n] = x
        return carry

    lax.fori_loop(0, slots // unroll, body, 0)


def drop_single(pool):
    return pool.reshape(pool.shape[0], pool.shape[1], pool.shape[3]) if pool.shape[2] == 1 else pool


def attend(query_rows, fresh_rows, pool, table, count, steps, copies, unroll):
    slots, rows, head_dim = query_rows.shape
    blocks = table.shape[1]
    dims = (slots, blocks, steps, rows // steps, copies, unroll)
    part = pool.shape[:-1] + (head_dim,)
    return pl.pallas_call(
        functools.partial(attend_kernel, dims),
        out_shape=jax.ShapeDtypeStruct((slots, rows, head_dim), jnp.bfloat16),
        in_specs=[SMEM, SMEM, VMEM, VMEM, ANY],
        out_specs=VMEM,
        scratch_shapes=[
            pltpu.VMEM(part, jnp.bfloat16),
            pltpu.VMEM(part, jnp.bfloat16),
            pltpu.SemaphoreType.DMA((2,)),
        ],
        compiler_params=pltpu.CompilerParams(vmem_limit_bytes=VMEM_ASK),
        cost_estimate=pl.CostEstimate(
            flops=4 * slots * rows * 336 * head_dim, bytes_accessed=4 * pool.size, transcendentals=slots * rows * 336
        ),
    )(table, count, query_rows, fresh_rows, pool)


def moved_kernel(dims, slot_ref, query_ref, fresh_ref, main_ref, *refs):
    blocks, steps, heads, copies = dims
    got_refs, out_ref = refs[:-1], refs[-1]
    moves = range(len(got_refs))
    head_dim = query_ref.shape[-1]
    rows = steps * heads
    cached = blocks * got_refs[0].shape[1]
    limit = masks(rows, heads, copies, cached, cached + fresh_ref.shape[1])
    out_ref[...] = main_ref[...]
    ids = [jnp.maximum(slot_ref[j], 0) for j in moves]

    def rows_of(j, lo):
        found = [got_refs[j][b, :, lo : lo + head_dim] for b in range(blocks)]
        return jnp.concatenate(found + [fresh_ref[ids[j], :, lo : lo + head_dim]], axis=0)

    bounds = [
        got_refs[j][blocks, :, 0:head_dim].astype(jnp.float32)[0:1, 0:1].astype(jnp.int32) * copies
        for j in moves
    ]
    heads_of = attend_group(
        [query_ref[n] for n in ids],
        [rows_of(j, 0) for j in moves],
        [rows_of(j, head_dim) for j in moves],
        bounds,
        limit,
    )
    for j in moves:

        @pl.when(slot_ref[j] >= 0)
        def _():
            out_ref[ids[j]] = heads_of[j]


def attend_moved(query_rows, fresh_rows, got, to_slot, main, blocks, steps, copies):
    rows = query_rows.shape[1]
    dims = (blocks, steps, rows // steps, copies)
    return pl.pallas_call(
        functools.partial(moved_kernel, dims),
        out_shape=jax.ShapeDtypeStruct(main.shape, main.dtype),
        in_specs=[SMEM, VMEM, VMEM, VMEM] + [VMEM] * len(got),
        out_specs=VMEM,
    )(to_slot, query_rows, fresh_rows, main, *got)


def pack_kernel(blocks, head_dim, table_ref, chosen_ref, size_ref, pool_ref, *refs):
    out_refs, (keys, values, sems) = refs[:-3], refs[-3:]
    copies = []
    for j in range(len(out_refs)):
        for b in range(blocks):
            at = j * blocks + b
            block = pool_ref.at[table_ref[chosen_ref[j], b]]
            for half, store in enumerate((keys, values)):
                part = block.at[..., pl.ds(half * head_dim, head_dim)]
                copies.append(pltpu.make_async_copy(part, store.at[at], sems.at[2 * at + half]))
                copies[-1].start()
    shape = out_refs[0].shape[1:]
    for j, out_ref in enumerate(out_refs):
        size = jnp.full(shape, size_ref[chosen_ref[j]], jnp.int32)
        out_ref[blocks] = size.astype(jnp.float32).astype(jnp.bfloat16)
    for copy in copies:
        copy.wait()
    for j, out_ref in enumerate(out_refs):
        for b in range(blocks):
            for half, store in enumerate((keys, values)):
                cols = pl.ds(half * head_dim, head_dim)
                out_ref[b, :, cols] = store[j * blocks + b].reshape(shape[0], head_dim)


def pack(pool, table, chosen, sizes, copies):
    blocks = table.shape[1]
    moves = chosen.shape[0]
    head_dim = pool.shape[-1] // 2
    part = (moves * blocks,) + pool.shape[1:-1] + (head_dim,)
    out = jax.ShapeDtypeStruct((blocks + 1, pool.shape[1] * copies, 2 * head_dim), pool.dtype)
    return pl.pallas_call(
        functools.partial(pack_kernel, blocks, head_dim),
        out_shape=(out,) * moves,
        in_specs=[SMEM, SMEM, SMEM, ANY],
        out_specs=(VMEM,) * moves,
        scratch_shapes=[
            pltpu.VMEM(part, pool.dtype),
            pltpu.VMEM(part, pool.dtype),
            pltpu.SemaphoreType.DMA((2 * moves * blocks,)),
        ],
        compiler_params=pltpu.CompilerParams(vmem_limit_bytes=VMEM_ASK),
    )(table, chosen, sizes, pool)


def project_kernel(ranks, head_ref, keep_ref, resid_ref, w_ref, hidden_ref, scale_ref,
                   weight, sib_out, sib_in, y_out, y_in, whole, w_sem, s_send, s_recv, y_send, y_recv,
                   g_send, g_recv, h_send, h_recv, resid_here, resid_sem, out_sem):
    rows, width = hidden_ref.shape
    get_resid = pltpu.make_async_copy(resid_ref, resid_here, resid_sem.at[0])
    tall = ranks // 2
    pieces = width // ranks // CHUNK
    me = lax.axis_index("tensor")
    level = me // 2
    core = me % 2
    sibling = level * 2 + 1 - core

    def place(side, at_level, k):
        return (side * tall + at_level) * pieces + k

    def peer(off):
        return lax.rem(level + off, tall) * 2 + core

    barrier = pltpu.get_barrier_semaphore()
    pl.semaphore_signal(barrier, inc=1, device_id={"tensor": sibling}, device_id_type=MESH)
    for off in range(1, tall):
        pl.semaphore_signal(barrier, inc=1, device_id={"tensor": peer(off)}, device_id_type=MESH)

    def fetch(i, side):
        at_level = lax.rem(level + 1 + i // pieces, tall)
        chunk = place(side, at_level, lax.rem(i, pieces))
        slot = i * 2 + (0 if side is sib_side else 1)
        return pltpu.make_async_copy(
            w_ref.at[:, pl.ds(pl.multiple_of(chunk * CHUNK, CHUNK), CHUNK)], weight.at[slot], w_sem.at[slot]
        )

    sib_side = 1 - core
    steps = tall * pieces

    def start_fetch(i, carry):
        fetch(i, sib_side).start()
        fetch(i, core).start()
        return carry

    lax.fori_loop(0, steps, start_fetch, 0)
    get_resid.start()
    pl.semaphore_wait(barrier, tall)

    def to_sibling(i):
        return pltpu.make_async_remote_copy(
            sib_out.at[i], sib_in.at[i], s_send.at[i], s_recv.at[i],
            device_id={"tensor": sibling}, device_id_type=MESH)

    def to_peer(i):
        off = 1 + i // pieces
        return pltpu.make_async_remote_copy(
            y_out.at[i], y_in.at[i], y_send.at[i], y_recv.at[i],
            device_id={"tensor": peer(off)}, device_id_type=MESH)

    def gather_peer(off, k):
        at = (off - 1) * pieces + k
        slot = place(core, level, k)
        return pltpu.make_async_remote_copy(
            whole.at[slot], whole.at[slot], g_send.at[at], g_recv.at[at],
            device_id={"tensor": peer(off)}, device_id_type=MESH)

    def gather_wait(off, k):
        at = (off - 1) * pieces + k
        slot = place(core, lax.rem(level + tall - off, tall), k)
        return slot, pltpu.make_async_remote_copy(
            whole.at[slot], whole.at[slot], g_send.at[at], g_recv.at[at],
            device_id={"tensor": peer(off)}, device_id_type=MESH)

    def hand_over(side, off, k):
        at = off * pieces + k
        slot = place(side, lax.rem(level + tall - off, tall), k)
        return slot, pltpu.make_async_remote_copy(
            whole.at[slot], whole.at[slot], h_send.at[at], h_recv.at[at],
            device_id={"tensor": sibling}, device_id_type=MESH)

    def products(i):
        fetch(i, sib_side).wait()
        sib_out[i] = jnp.dot(
            head_ref[...], weight[i * 2], preferred_element_type=jnp.float32
        ).astype(jnp.bfloat16)
        to_sibling(i).start()
        fetch(i, core).wait()
        mine = jnp.dot(head_ref[...], weight[i * 2 + 1], preferred_element_type=jnp.float32)
        to_sibling(i).wait_recv()
        return mine + sib_in[i].astype(jnp.float32)

    def far(i, carry):
        y_out[i] = products(i).astype(jnp.bfloat16)
        to_peer(i).start()
        return carry

    lax.fori_loop(0, steps - pieces, far, 0)

    get_resid.wait()

    def near(k, carry):
        mixed = products(steps - pieces + k)
        for off in range(1, tall):
            at = (off - 1) * pieces + k
            to_peer(at).wait_recv()
            mixed = mixed + y_in[at].astype(jnp.float32)
        slot = place(core, level, k)
        cols = pl.ds(pl.multiple_of(slot * CHUNK, CHUNK), CHUNK)
        total = resid_here[:, cols].astype(jnp.float32) + mixed
        whole[slot] = jnp.where(keep_ref[...] > 0.0, total, 0.0).astype(jnp.bfloat16)
        for off in range(1, tall):
            gather_peer(off, k).start()
        hand_over(core, 0, k)[1].start()
        return carry

    lax.fori_loop(0, pieces, near, 0)

    def square(slot):
        wide = whole[slot].astype(jnp.float32)
        return jnp.sum(wide * wide, axis=-1, keepdims=True)

    squares = jnp.zeros((rows, 1), jnp.float32)
    for k in range(pieces):
        squares = squares + square(place(core, level, k))
        slot, copy = hand_over(sib_side, 0, k)
        copy.wait_recv()
        squares = squares + square(slot)
    for k in range(pieces):
        for off in range(1, tall):
            slot, copy = gather_wait(off, k)
            copy.wait_recv()
            hand_over(core, off, k)[1].start()
            squares = squares + square(slot)
    for k in range(pieces):
        for off in range(1, tall):
            slot, copy = hand_over(sib_side, off, k)
            copy.wait_recv()
            squares = squares + square(slot)
    scale_ref[...] = lax.rsqrt(squares * (1.0 / width) + 1e-05)
    stores = [
        pltpu.make_async_copy(whole.at[j], hidden_ref.at[:, pl.ds(j * CHUNK, CHUNK)], out_sem.at[j])
        for j in range(width // CHUNK)
    ]
    for store in stores:
        store.start()
    for i in range(steps):
        to_sibling(i).wait_send()
    for i in range(steps - pieces):
        to_peer(i).wait_send()
    for k in range(pieces):
        hand_over(core, 0, k)[1].wait_send()
        for off in range(1, tall):
            gather_peer(off, k).wait_send()
            hand_over(core, off, k)[1].wait_send()
    for store in stores:
        store.wait()


def project(flat_heads, keep_rows, resid_rows, w_out, ranks):
    rows = flat_heads.shape[0]
    depth, width = w_out.shape
    pieces = width // ranks // CHUNK
    steps = ranks // 2 * pieces
    far = steps - pieces
    block = (rows, CHUNK)
    dma = pltpu.SemaphoreType.DMA
    out = jax.ShapeDtypeStruct((rows, width), jnp.bfloat16)
    return pl.pallas_call(
        functools.partial(project_kernel, ranks),
        out_shape=(out, jax.ShapeDtypeStruct((rows, 1), jnp.float32)),
        in_specs=[VMEM, VMEM, ANY, ANY],
        out_specs=(ANY, VMEM),
        scratch_shapes=[
            pltpu.VMEM((2 * steps, depth, CHUNK), jnp.bfloat16),
            pltpu.VMEM((steps,) + block, jnp.bfloat16),
            pltpu.VMEM((steps,) + block, jnp.bfloat16),
            pltpu.VMEM((far,) + block, jnp.bfloat16),
            pltpu.VMEM((far,) + block, jnp.bfloat16),
            pltpu.VMEM((2 * steps,) + block, jnp.bfloat16),
            dma((2 * steps,)),
            dma((steps,)), dma((steps,)),
            dma((far,)), dma((far,)),
            dma((far,)), dma((far,)),
            dma((steps,)), dma((steps,)),
            pltpu.VMEM((rows, width), jnp.bfloat16), dma((1,)), dma((2 * steps,)),
        ],
        compiler_params=pltpu.CompilerParams(
            collective_id=0, has_side_effects=True, vmem_limit_bytes=56 * 2**20
        ),
        cost_estimate=pl.CostEstimate(
            flops=2 * rows * depth * width, bytes_accessed=2 * depth * width, transcendentals=0
        ),
    )(flat_heads, keep_rows, resid_rows, w_out)


def norm_kernel(hidden_ref, scale_ref, gain_ref, same_ref, normed_ref):
    hidden = hidden_ref[...]
    same_ref[...] = hidden
    gain = gain_ref[...].astype(jnp.float32)
    normed_ref[...] = (hidden.astype(jnp.float32) * scale_ref[...] * gain).astype(jnp.bfloat16)


def norm(hidden, scale, gain):
    rows, width = hidden.shape
    cols = 1024
    block = pl.BlockSpec((rows, cols), lambda i: (0, i))
    out = jax.ShapeDtypeStruct((rows, width), jnp.bfloat16)
    return pl.pallas_call(
        norm_kernel,
        grid=(width // cols,),
        out_shape=(out, out),
        in_specs=[block, pl.BlockSpec((rows, 1), lambda i: (0, 0)), pl.BlockSpec((1, cols), lambda i: (0, i))],
        out_specs=(block, block),
    )(hidden, scale, gain)


def per_device(replicas, ranks, queries, new_kv, pool, lengths, block_table, plan, w_out, residual, norm_gain):
    my_replica = lax.axis_index("replica")
    steps, slots, _ = queries.shape
    head_dim = pool.shape[3] // 2
    copies = pool.shape[2]
    heads = queries.shape[2] // head_dim
    blocks = block_table.shape[1]
    width = w_out.shape[1]
    source_slot, source, target, target_slot = (plan[:, i] for i in range(4))
    slot_ids = jnp.arange(slots, dtype=jnp.int32)
    sending = source == my_replica
    arriving = target == my_replica
    shifts = jnp.arange(1, replicas, dtype=jnp.int32)
    leaving = sending[None, :] & (target[None, :] == ((my_replica + shifts) % replicas)[:, None])
    chosen = jnp.sum(jnp.where(leaving, source_slot[None, :], 0), axis=1)
    pool = drop_single(pool)
    got = [
        lax.ppermute(block, "replica", [(r, (r + d) % replicas) for r in range(replicas)])
        for d, block in enumerate(pack(pool, block_table, chosen, lengths, copies), 1)
    ]

    query_rows = queries.reshape(steps, slots, heads, head_dim).transpose(1, 0, 2, 3)
    query_rows = query_rows.reshape(slots, steps * heads, head_dim)
    fresh_rows = new_kv.transpose(1, 0, 2, 3).reshape(slots, steps * copies, 2 * head_dim)
    fresh_rows = jnp.pad(fresh_rows, ((0, 0), (0, 16 - steps * copies), (0, 0)))
    main = attend(query_rows, fresh_rows, pool, block_table, lengths, steps, copies, 8)

    arrival = arriving[None, :] & (source[None, :] == ((my_replica - shifts) % replicas)[:, None])
    to_slot = jnp.sum(jnp.where(arrival, target_slot[None, :] + 1, 0), axis=1) - 1
    head_out = attend_moved(query_rows, fresh_rows, got, to_slot, main, blocks, steps, copies)
    flat_heads = head_out.reshape(slots, steps, heads * head_dim).transpose(1, 0, 2)
    flat_heads = flat_heads.reshape(steps * slots, heads * head_dim)

    incoming = jnp.any(arriving[None, :] & (target_slot[None, :] == slot_ids[:, None]), axis=1)
    moved_out = jnp.any(sending[None, :] & (source_slot[None, :] == slot_ids[:, None]), axis=1)
    live = incoming | (lengths > 0) & jnp.logical_not(moved_out)
    keep_rows = jnp.tile(live, steps)[:, None].astype(jnp.float32)
    resid_rows = residual.reshape(steps * slots, width)
    hidden, scale = project(flat_heads, keep_rows, resid_rows, w_out, ranks)
    hidden, normed = norm(hidden, scale, norm_gain[None, :])
    out_shape = (steps, slots, width)
    return (hidden.reshape(out_shape), normed.reshape(out_shape))


def solution(mesh):
    in_specs = (
        P(None, ("groups", "replica"), "tensor"),
        P(None, ("groups", "replica"), "tensor", None),
        P(("groups", "replica"), None, "tensor", None),
        P(("groups", "replica")),
        P(("groups", "replica"), None),
        P("groups", None),
        P("tensor", None),
        P(None, ("groups", "replica"), None),
        P(),
    )
    out_specs = (P(None, ("groups", "replica"), None), P(None, ("groups", "replica"), None))
    return jax.shard_map(
        functools.partial(per_device, mesh.shape["replica"], mesh.shape["tensor"]),
        mesh=mesh, in_specs=in_specs, out_specs=out_specs, check_vma=False,
    )
```
